256 devices in a mesh: dp: 16 (over z, core), tp: 16 (over x, y).
Axes of the slice: x: 4, y: 4, z: 8, core: 2. Of those that a mesh axis runs over, the one named last changes fastest.
Arguments:
- latent_cache: bfloat16 [1024, 1024, 576], P(('dp', 'tp')), may hold values from -5 to 5
- lengths: int32 [1024], P(('dp', 'tp')), may hold values from 1 to 1022, as said below
- queries: bfloat16 [2, 1024, 128, 576], P(None, ('dp', 'tp')), may hold values from -45 to 45
- new_latents: bfloat16 [2, 1024, 576], P(None, ('dp', 'tp')), may hold values from -5.4 to 5.4
- migrations: int32 [256, 2], P(('dp', 'tp')), may hold values from 0 to 15, as said below
- value_weight: bfloat16 [128, 512, 128], P('tp'), may hold values from -0.25 to 0.25
- output_weight: bfloat16 [16384, 7168], P('tp', 'dp'), may hold values from -0.046875 to 0.046875
Outputs:
- projected: bfloat16 [2560, 7168], P('tp', 'dp')
The draws below stay inside these ranges and needn't reach their ends.
Inputs may be any that keep to these rules, and one draw needn't show every extreme that they name: `lengths`: A request that migrates holds at most 256 cached positions; in every draw one holds exactly 256, another request exactly 1022, another exactly 1. migrations[d, 0] is 4 where device d hands nothing away; migrations[d, 1] then means nothing. A request moves only between devices of the same tp index and to another dp index; each device takes at most one request; every tp index has a device that hands one away.
All inputs are finite; a program needn't handle non-finite values.
Results may differ from the reference program's by a relative error of at most 0.019.
Values may be sent and summed in bfloat16 or wider, within the bound.
No kernel may reach another device: no remote copies, remote signals or barrier semaphores. Data moves between devices by JAX's collectives and lax.ppermute only.
A program may use at most 64 MiB of HBM per device.

```python
import math
import jax
import jax.numpy as jnp
from jax import lax

H = 128
NOPE = 128
ROPE = 64
VAL = 512
HEAD = 128
DM = 7168
REQ_DEV = 4
CAP = 1024
STEPS = 2
LATENT = 576
MIG_TOK = 256
ROWS_OUT = 5
REQUESTS = 1024
ALLROWS = 2560
N_DP = 16
N_TP = 16
DEVICES = 256


def migration_plan(key):
    keys = jax.random.split(key, 6)
    order = jax.vmap(lambda single: jax.random.permutation(single, N_DP))(jax.random.split(keys[0], N_TP))
    column = jnp.arange(N_TP)[:, None]
    target = jnp.zeros((N_TP, N_DP), jnp.int32).at[column, order].set(jnp.roll(order, -1, axis=1))
    leader = jnp.arange(N_DP)[None, :] == order[:, :1]
    moving = (jax.random.randint(keys[1], (N_TP, N_DP), 0, 2) == 1) | leader
    chosen_slot = jax.random.randint(keys[2], (N_TP, N_DP), 0, REQ_DEV)
    target = target.T.reshape(DEVICES)
    leader = leader.T.reshape(DEVICES)
    moving = moving.T.reshape(DEVICES)
    chosen_slot = chosen_slot.T.reshape(DEVICES)
    longest = CAP - STEPS
    factor = jax.random.randint(keys[3], (DEVICES, 1), 1, 5)
    resident = 1 + jax.random.randint(keys[4], (DEVICES, REQ_DEV), 0, longest) * factor // 4
    migrant = jax.random.randint(keys[5], (DEVICES, REQ_DEV), 1, MIG_TOK + 1)
    position = jnp.arange(REQ_DEV)[None, :]
    at_slot = position == chosen_slot[:, None]
    counts = jnp.where(moving[:, None] & at_slot, migrant, resident)
    counts = jnp.where(leader[:, None] & at_slot, MIG_TOK, counts)
    counts = jnp.where(leader[:, None] & (position == (chosen_slot[:, None] + 1) % REQ_DEV), longest, counts)
    counts = jnp.where(leader[:, None] & (position == (chosen_slot[:, None] + 2) % REQ_DEV), 1, counts)
    plan = jnp.stack([jnp.where(moving, chosen_slot, REQ_DEV), target], axis=1)
    return (counts.reshape(REQUESTS).astype(jnp.int32), plan.astype(jnp.int32))


def latent_base(key):
    return jnp.clip(jax.random.normal(key, (STEPS, REQUESTS, LATENT), jnp.float32), -4.5, 4.5)


def draw_lengths(key, part):
    counts, plan = migration_plan(key)
    return counts


def draw_migrations(key, part):
    counts, plan = migration_plan(key)
    return plan


def draw_new_latents(key, part):
    base = latent_base(key)
    return base.astype(jnp.bfloat16)


def draw_queries(key, part):
    key = jax.random.fold_in(key, 12)
    keys = jax.random.split(key, 1)
    fresh = jnp.clip(jax.random.normal(keys[0], (STEPS, REQUESTS, H, LATENT), jnp.float32), -6.0, 6.0)
    return fresh.astype(jnp.bfloat16)


def block_levels(key, shape, pieces, smallest, top_value):
    gain = 1.0
    for axis_at, parts in pieces:
        steps = jax.random.uniform(jax.random.fold_in(jax.random.fold_in(key, 6), axis_at), (parts,), jnp.float32, smallest / len(pieces), top_value / len(pieces))
        gain = gain * jnp.repeat(jnp.exp(steps), shape[axis_at] // parts).reshape((-1,) + (1,) * (len(shape) - 1 - axis_at))
    return gain


def noise(own_key, shape, scale, limit, cuts=(), kind=jnp.bfloat16):
    level = block_levels(own_key, shape, cuts, -0.22, 0.18) if cuts else 1.0
    values = jax.random.normal(own_key, shape, jnp.float32) * scale * level
    return jnp.minimum(jnp.maximum(values, -limit), limit).astype(kind)


def setup_inputs(seed: int = 0) -> dict:
    streams_of = jax.random.split(jax.random.key(seed), 8)
    return {
        "latent_cache": noise(streams_of[0], (REQUESTS, CAP, LATENT), 1.0, 5.0, ((0, 256),)),
        "lengths": draw_lengths(jax.random.fold_in(streams_of[7], 71), 0),
        "queries": draw_queries(jax.random.fold_in(streams_of[7], 71), 0),
        "new_latents": draw_new_latents(jax.random.fold_in(streams_of[7], 71), 0),
        "migrations": draw_migrations(jax.random.fold_in(streams_of[7], 71), 0),
        "value_weight": noise(streams_of[5], (H, VAL, HEAD), VAL ** -0.5, 0.25, ((0, 16),)),
        "output_weight": noise(streams_of[6], (H * HEAD, DM), (H * HEAD) ** -0.5, 0.046875, ((0, 16), (1, 16))),
    }


def attend_one(request_query, request_cache, request_new, filled):
    scaling = 1.0 / math.sqrt(NOPE + ROPE)
    query_wide = request_query.astype(jnp.float32)
    far_scores = jnp.einsum('shl,cl->shc', query_wide, request_cache.astype(jnp.float32)) * scaling
    own_scores = jnp.einsum('shl,tl->sht', query_wide, request_new.astype(jnp.float32)) * scaling
    step_count = request_query.shape[0]
    far_mask = (jnp.arange(request_cache.shape[0]) < filled)[None, None, :]
    own_mask = (jnp.arange(step_count)[None, :] <= jnp.arange(step_count)[:, None])[:, None, :]
    highest = jnp.maximum(lax.optimization_barrier(jnp.max(jnp.where(far_mask, far_scores, -jnp.inf), axis=2)), lax.optimization_barrier(jnp.max(jnp.where(own_mask, own_scores, -jnp.inf), axis=2)))
    far_weights = jnp.where(far_mask, jnp.exp(far_scores - highest[:, :, None]), 0.0)
    own_weights = jnp.where(own_mask, jnp.exp(own_scores - highest[:, :, None]), 0.0)
    denominator = lax.optimization_barrier(jnp.sum(far_weights, axis=2)) + lax.optimization_barrier(jnp.sum(own_weights, axis=2))
    far_rounded = lax.optimization_barrier(far_weights.astype(jnp.bfloat16)).astype(jnp.float32)
    own_rounded = lax.optimization_barrier(own_weights.astype(jnp.bfloat16)).astype(jnp.float32)
    weighted = jnp.einsum('shc,cv->shv', far_rounded, request_cache[:, :VAL].astype(jnp.float32))
    weighted = weighted + jnp.einsum('sht,tv->shv', own_rounded, request_new[:, :VAL].astype(jnp.float32))
    return (weighted / denominator[:, :, None]).astype(jnp.bfloat16)

def attend_packed(packed):
    return attend_one(packed[0], packed[1], packed[2], packed[3])

def reference(latent_cache, lengths, queries, new_latents, migrations, value_weight, output_weight):
    request_query = jnp.swapaxes(queries, 0, 1)
    request_new = jnp.swapaxes(new_latents, 0, 1)
    latent_out = lax.map(attend_packed, (request_query, latent_cache, request_new, lengths))
    by_device = latent_out.reshape(DEVICES, REQ_DEV, STEPS, H, VAL)
    outward = migrations[:, 0]
    target = migrations[:, 1]
    leaving = outward < REQ_DEV
    picked = jnp.minimum(outward, REQ_DEV - 1).astype(jnp.int32)
    retained = (jnp.arange(REQ_DEV)[None, :] != outward[:, None]).astype(by_device.dtype)
    retained_rows = by_device * retained[:, :, None, None, None]
    leaving_rows = jnp.take_along_axis(by_device, picked[:, None, None, None, None], axis=1)[:, 0]
    device_ids = jnp.arange(DEVICES, dtype=jnp.int32)
    dp_index = device_ids // N_TP
    tp_index = device_ids % N_TP
    matches = leaving[:, None] & (tp_index[:, None] == tp_index[None, :]) & (target[:, None] == dp_index[None, :])
    matches = matches.astype(jnp.int32)
    present = lax.optimization_barrier(jnp.sum(matches, axis=0))
    source = lax.optimization_barrier(jnp.sum(matches * device_ids[:, None], axis=0)).astype(jnp.int32)
    inbound = leaving_rows[source] * present[:, None, None, None].astype(by_device.dtype)
    slot_rows = jnp.concatenate([retained_rows, inbound[:, None]], axis=1)
    placed = slot_rows.reshape(N_DP, N_TP, ROWS_OUT, STEPS, H, VAL).transpose(0, 3, 1, 2, 4, 5)
    placed = placed.reshape(ALLROWS, H, VAL)
    hidden = jnp.einsum('rhv,hvd->rhd', placed.astype(jnp.float32), value_weight.astype(jnp.float32))
    hidden = hidden.astype(jnp.bfloat16).reshape(ALLROWS, H * HEAD)
    return jnp.dot(hidden, output_weight, preferred_element_type=jnp.float32).astype(jnp.bfloat16)
```

```python
import math

import jax
import jax.numpy as jnp
from jax import lax
from jax.experimental import pallas as pl
from jax.experimental.pallas import tpu as pltpu
from jax.sharding import PartitionSpec as P

NOPE = 128
ROPE = 64
VAL = 512
HEAD = 128
REQ = 4
STEPS = 2
N = 16
GROUP = 8
HOME = N * REQ * STEPS
OUT = HOME + N * STEPS
META = 16
F32 = jnp.float32
BF16 = jnp.bfloat16
SCALE = 1.0 / math.sqrt(NOPE + ROPE) * math.log2(math.e)


def attend_kernel(lengths, moves, query, cache, new, out):
    k = pl.program_id(0)

    @pl.when(k < REQ)
    def _():
        rows = STEPS * N * GROUP
        q = query[...].reshape(rows, cache.shape[2])
        keys = cache[0]
        own = new[0]
        dims = (((1,), (1,)), ((), ()))
        far = lax.dot_general(q, keys, dims, preferred_element_type=F32)
        near = lax.dot_general(q, own, dims, preferred_element_type=F32)
        filled = lengths[jnp.minimum(k, REQ - 1)]
        far_ok = lax.broadcasted_iota(jnp.int32, (1, keys.shape[0]), 1) < filled
        step = lax.broadcasted_iota(jnp.int32, near.shape, 0) // (N * GROUP)
        near_ok = lax.broadcasted_iota(jnp.int32, near.shape, 1) <= step
        far = jnp.where(far_ok, far, -jnp.inf)
        near = jnp.where(near_ok, near, -jnp.inf)
        top = jnp.maximum(
            jnp.max(far, axis=1, keepdims=True), jnp.max(near, axis=1, keepdims=True)
        )
        far = jnp.exp2((far - top) * SCALE)
        near = jnp.exp2((near - top) * SCALE)
        total = jnp.sum(far, axis=1, keepdims=True) + jnp.sum(near, axis=1, keepdims=True)
        mixed = jnp.dot(far.astype(BF16), keys[:, :VAL], preferred_element_type=F32)
        mixed = mixed + jnp.dot(near.astype(BF16), own[:, :VAL], preferred_element_type=F32)
        mixed = mixed / total
        half = N * GROUP
        out[...] = jnp.concatenate(
            [mixed[:half].reshape(N, GROUP, VAL), mixed[half:].reshape(N, GROUP, VAL)], axis=1
        ).astype(BF16)

    @pl.when(k == REQ)
    def _():
        lane = lax.broadcasted_iota(jnp.int32, out.shape, 2)
        out[...] = jnp.where(lane < 128, moves[0, 1], moves[0, 0]).astype(F32).astype(BF16)


def attend(lengths, moves, queries, cache, new):
    width = cache.shape[2]
    last = REQ - 1
    return pl.pallas_call(
        attend_kernel,
        grid_spec=pltpu.PrefetchScalarGridSpec(
            num_scalar_prefetch=2,
            grid=(REQ + 1,),
            in_specs=[
                pl.BlockSpec(
                    (STEPS, 1, N * GROUP, width), lambda k, *_: (0, jnp.minimum(k, last), 0, 0)
                ),
                pl.BlockSpec(
                    (1, cache.shape[1], width), lambda k, *_: (jnp.minimum(k, last), 0, 0)
                ),
                pl.BlockSpec((1, META, width), lambda k, *_: (jnp.minimum(k, last), 0, 0)),
            ],
            out_specs=pl.BlockSpec((N, STEPS * GROUP, VAL), lambda k, *_: (0, k, 0)),
        ),
        out_shape=jax.ShapeDtypeStruct((N, (REQ + 1) * STEPS * GROUP, VAL), BF16),
        compiler_params=pltpu.CompilerParams(vmem_limit_bytes=48 * 2**20),
    )(lengths, moves, queries, cache, new)


def value_kernel(mine, got, weight, out, wide):
    body = REQ * STEPS * GROUP
    pieces = VAL // 128
    for p in range(pieces):
        wide[p] = got[:, :body, p * 128 : (p + 1) * 128].astype(F32).reshape(N * body, 128)
    for h in range(GROUP):
        rows = jnp.concatenate(
            [wide[p, pl.ds(h, HOME, stride=GROUP), :] for p in range(pieces)], axis=1
        ).astype(BF16)
        out[:HOME, h * HEAD : (h + 1) * HEAD] = jnp.dot(
            rows, weight[h], preferred_element_type=F32
        ).astype(BF16)
    lane = lax.broadcasted_iota(jnp.int32, (N, 256), 1)
    moves = got[:, body : body + META, :256].astype(F32)[:, 0, :]
    ours = (lane % 128) // (REQ * STEPS) == mine[0]
    out[HOME:, :] = jnp.zeros((META, out.shape[1]), BF16)
    out[HOME:, :256] = jnp.where(ours, moves, 0.0).astype(BF16)


def values(mine, got, weight):
    return pl.pallas_call(
        value_kernel,
        in_specs=[
            pl.BlockSpec(memory_space=pltpu.SMEM),
            pl.BlockSpec(memory_space=pltpu.VMEM),
            pl.BlockSpec(memory_space=pltpu.VMEM),
        ],
        out_specs=pl.BlockSpec(memory_space=pltpu.VMEM),
        out_shape=jax.ShapeDtypeStruct((HOME + META, GROUP * HEAD), BF16),
        scratch_shapes=[pltpu.VMEM((VAL // 128, N * REQ * STEPS * GROUP, 128), F32)],
        compiler_params=pltpu.CompilerParams(vmem_limit_bytes=48 * 2**20),
    )(mine, got, weight)


def project_kernel(order, *refs):
    blocks, weight, out, held = refs[:N], refs[N], refs[N + 1], refs[N + 2]
    cell = REQ * STEPS
    table = jnp.zeros((N, 256), F32)
    for b in range(N):
        part = jnp.dot(blocks[b][:HOME, :], weight[...], preferred_element_type=F32)
        row = pl.multiple_of(order[b] * cell, cell)
        held[:, pl.ds(row, cell), :] = part.reshape(N, cell, part.shape[1])
        table = table + blocks[b][HOME:, :256].astype(F32)
    table = table.astype(jnp.int32)
    wide = (HOME, HOME)
    r = lax.broadcasted_iota(jnp.int32, wide, 0)
    c = lax.broadcasted_iota(jnp.int32, wide, 1)
    slot_c = (c % cell) // STEPS
    same_step = r % STEPS == c % STEPS
    per = 4
    arriving = None
    kept = None
    for j in range(N):
        rows = held[j].astype(BF16)
        target = table[j : j + 1, :HOME]
        slot = table[j : j + 1, HOME : 2 * HOME]
        moved = slot_c == slot
        keep = ((r == c) & ~moved).astype(F32).astype(BF16)
        here = (r // cell == target) & moved & same_step & ((r % cell) // STEPS == j % per)
        mine = jnp.dot(keep, rows, preferred_element_type=F32).reshape(N, cell, -1)
        came = jnp.dot(here.astype(F32).astype(BF16), rows, preferred_element_type=F32)
        arriving = came if j % per == 0 else arriving + came
        if j % 2 == 0:
            kept = mine
        else:
            out[:, (j - 1) * cell : (j + 1) * cell, :] = jnp.concatenate([kept, mine], axis=1).astype(BF16)
        if j % (2 * per) == per - 1:
            first = arriving
        if j % (2 * per) == 2 * per - 1:
            both = jnp.concatenate(
                [first.reshape(N, cell, -1), arriving.reshape(N, cell, -1)], axis=1
            )
            at = HOME + (j // (2 * per)) * 2 * cell
            out[:, at : at + 2 * cell, :] = both.astype(BF16)


def project(order, blocks, weight):
    cols = weight.shape[1]
    vmem = pl.BlockSpec(memory_space=pltpu.VMEM)
    return pl.pallas_call(
        project_kernel,
        in_specs=[pl.BlockSpec(memory_space=pltpu.SMEM)] + [vmem] * (N + 1),
        out_specs=vmem,
        out_shape=jax.ShapeDtypeStruct((N, OUT, cols), BF16),
        scratch_shapes=[pltpu.VMEM((N, HOME, cols), F32)],
        compiler_params=pltpu.CompilerParams(vmem_limit_bytes=48 * 2**20),
    )(order, *blocks, weight)


def finish_kernel(got, out):
    total = got[0].astype(F32)
    for j in range(1, N):
        total = total + got[j].astype(F32)
    rows = total.astype(BF16)
    o = lax.broadcasted_iota(jnp.int32, (OUT, OUT), 0)
    c = lax.broadcasted_iota(jnp.int32, (OUT, OUT), 1)
    slots = REQ + 1
    step, j, slot = o // (N * slots), (o // slots) % N, o % slots
    source = jnp.where(
        slot < REQ, j * (REQ * STEPS) + slot * STEPS + step, HOME + j * STEPS + step
    )
    pick = (c == source).astype(F32).astype(BF16)
    out[...] = jnp.dot(pick, rows, preferred_element_type=F32).astype(BF16)


def finish(got):
    return pl.pallas_call(
        finish_kernel,
        in_specs=[pl.BlockSpec(memory_space=pltpu.VMEM)],
        out_specs=pl.BlockSpec(memory_space=pltpu.VMEM),
        out_shape=jax.ShapeDtypeStruct(got.shape[1:], BF16),
        compiler_params=pltpu.CompilerParams(vmem_limit_bytes=48 * 2**20),
    )(got)


def along_z(by):
    chips = N // 2
    return [(z * 2 + c, (z + by) % chips * 2 + c) for z in range(chips) for c in range(2)]


OTHER_CORE = [(i, i ^ 1) for i in range(N)]


def gather(block):
    me = lax.axis_index("dp")
    chips = N // 2
    held = [(block, me)]
    up = down = block
    for hop in range(1, chips // 2 + 1):
        up = lax.ppermute(up, "dp", along_z(1))
        held.append((up, (me + N - 2 * hop) % N))
        if hop < chips // 2:
            down = lax.ppermute(down, "dp", along_z(-1))
            held.append((down, (me + 2 * hop) % N))
    held += [(lax.ppermute(b, "dp", OTHER_CORE), i ^ 1) for b, i in held]
    return [b for b, _ in held], jnp.stack([i for _, i in held]).astype(jnp.int32)


def shards(latent_cache, lengths, queries, new_latents, migrations, value_weight, output_weight):
    leaving = migrations[:, 0] < REQ
    moves = jnp.stack([migrations[:, 0], jnp.where(leaving, migrations[:, 1], -1)], axis=1)
    new = jnp.pad(jnp.swapaxes(new_latents, 0, 1), ((0, 0), (0, META - STEPS), (0, 0)))
    sent = attend(lengths, moves, queries, latent_cache, new)
    got = lax.all_to_all(sent, "tp", split_axis=0, concat_axis=0, tiled=True)
    me = lax.axis_index("dp").astype(jnp.int32).reshape(1)
    hidden = values(me, got, value_weight)
    blocks, order = gather(hidden)
    partial = project(order, blocks, output_weight)
    shares = lax.all_to_all(partial, "tp", split_axis=0, concat_axis=0, tiled=True)
    return finish(shares)


def solution(mesh):
    return jax.shard_map(
        shards,
        mesh=mesh,
        in_specs=(
            P(("dp", "tp"), None, None),
            P(("dp", "tp")),
            P(None, ("dp", "tp"), None, None),
            P(None, ("dp", "tp"), None),
            P(("dp", "tp"), None),
            P("tp", None, None),
            P("tp", "dp"),
        ),
        out_specs=P("tp", "dp"),
        check_vma=False,
    )
```

```python
import math

import jax
import jax.numpy as jnp
from jax import lax
from jax.experimental import pallas as pl
from jax.experimental.pallas import tpu as pltpu
from jax.sharding import PartitionSpec as P

NOPE = 128
ROPE = 64
VAL = 512
HEAD = 128
REQ = 4
STEPS = 2
N = 16
GROUP = 8
META = 16
LANES = 128
CHUNKS = ((0, 4),)
ARRIVING = N * STEPS
TOGETHER = 2
F32 = jnp.float32
BF16 = jnp.bfloat16
SCALE = 1.0 / math.sqrt(NOPE + ROPE) * math.log2(math.e)
NT = (((1,), (1,)), ((), ()))


def attend_one(q, keys, own, filled):
    far = jnp.dot(q, keys, preferred_element_type=F32)
    near = lax.dot_general(q, own, NT, preferred_element_type=F32)
    far_ok = lax.broadcasted_iota(jnp.int32, (1, keys.shape[1]), 1) < filled
    step = lax.broadcasted_iota(jnp.int32, near.shape, 0) // (N * GROUP)
    near_ok = lax.broadcasted_iota(jnp.int32, near.shape, 1) <= step
    far = jnp.where(far_ok, far, -jnp.inf)
    near = jnp.where(near_ok, near, -jnp.inf)
    top = jnp.maximum(jnp.max(far, axis=1, keepdims=True), jnp.max(near, axis=1, keepdims=True))
    far = jnp.exp2((far - top) * SCALE)
    near = jnp.exp2((near - top) * SCALE)
    total = jnp.sum(far, axis=1, keepdims=True) + jnp.sum(near, axis=1, keepdims=True)
    mixed = lax.dot_general(far.astype(BF16), keys[:VAL], NT, preferred_element_type=F32)
    mixed = mixed + jnp.dot(near.astype(BF16), own[:, :VAL], preferred_element_type=F32)
    return mixed / total


def attend_kernel(lengths, moves, query, cache, new, out):
    half = N * GROUP
    rows = STEPS * GROUP
    body = REQ * rows
    turn = pl.program_id(0)
    for u in range(TOGETHER):
        request = turn * TOGETHER + u
        q = jnp.concatenate([query[s, u].T for s in range(STEPS)], axis=0)
        fresh = new[...].astype(F32)
        fresh = jnp.where(turn == 0, fresh[:, u, :], fresh[:, TOGETHER + u, :])
        own = jnp.concatenate([fresh, jnp.zeros((META - STEPS, fresh.shape[1]), F32)], axis=0)
        mixed = attend_one(q, cache[u], own.astype(BF16), lengths[request])
        mixed = jnp.concatenate(
            [mixed[:half].reshape(N, GROUP, VAL), mixed[half:].reshape(N, GROUP, VAL)], axis=1
        ).astype(BF16)
        for p in range(VAL // LANES):
            at = pl.multiple_of(p * body + request * rows, rows)
            out[:, pl.ds(at, rows), :] = mixed[:, :, p * LANES : (p + 1) * LANES]
    lane = lax.broadcasted_iota(jnp.int32, (N, META, LANES), 2)
    slot = moves[0, 0]
    taker = jnp.where(slot < REQ, moves[0, 1], -1)
    out[:, body * (VAL // LANES) :, :] = (
        jnp.where(lane < LANES // 2, taker, slot).astype(F32).astype(BF16)
    )


def attend(lengths, moves, queries, cache, new):
    width = cache.shape[1]
    rows = REQ * STEPS * GROUP * (VAL // LANES) + META
    return pl.pallas_call(
        attend_kernel,
        grid_spec=pltpu.PrefetchScalarGridSpec(
            num_scalar_prefetch=2,
            grid=(REQ // TOGETHER,),
            in_specs=[
                pl.BlockSpec((STEPS, TOGETHER, width, N * GROUP), lambda g, *_: (0, g, 0, 0)),
                pl.BlockSpec((TOGETHER, width, cache.shape[2]), lambda g, *_: (g, 0, 0)),
                pl.BlockSpec(new.shape, lambda g, *_: (0, 0, 0)),
            ],
            out_specs=pl.BlockSpec((N, rows, LANES), lambda g, *_: (0, 0, 0)),
        ),
        out_shape=jax.ShapeDtypeStruct((N, rows, LANES), BF16),
        compiler_params=pltpu.CompilerParams(vmem_limit_bytes=56 * 2**20),
    )(lengths, moves, queries, cache, new)


def value_kernel(got, weight, *refs):
    outs, wide = refs[:-1], refs[-1]
    body = REQ * STEPS * GROUP
    pieces = VAL // LANES
    moves = got[:, pieces * body :, :].astype(F32)[:, 0, :]
    sub = lax.broadcasted_iota(jnp.int32, (N, LANES), 0)
    lane = lax.broadcasted_iota(jnp.int32, (N, LANES), 1)
    taker = jnp.max(jnp.where(lane < LANES // 2, moves, -1.0), axis=1, keepdims=True)
    slot = jnp.max(jnp.where(lane < LANES // 2, -1.0, moves), axis=1, keepdims=True)
    parts = []
    for (first, count), out in zip(CHUNKS, outs, strict=True):
        cell = count * STEPS * GROUP
        home = N * count * STEPS
        for p in range(pieces):
            at = p * body + first * STEPS * GROUP
            wide[p, : N * cell, :] = got[:, at : at + cell, :].astype(F32).reshape(N * cell, LANES)
        for h in range(GROUP):
            rows = jnp.concatenate(
                [wide[p, pl.ds(h, home, stride=GROUP), :] for p in range(pieces)], axis=1
            ).astype(BF16)
            out[h * home : (h + 1) * home, :] = jnp.dot(
                rows, weight[h], preferred_element_type=F32
            ).astype(BF16)
        mine = lane // (count * STEPS) == sub
        for v in (taker, slot):
            parts.append(jnp.sum(jnp.where(mine, v, 0.0), axis=0, keepdims=True))
    row = lax.broadcasted_iota(jnp.int32, (META, LANES), 0)
    lines = jnp.zeros((META, LANES), F32)
    for i, part in enumerate(parts):
        lines = jnp.where(row == i, part, lines)
    out[GROUP * home :, :] = lines.astype(BF16)


def values(got, weight):
    homes = [N * count * STEPS for _, count in CHUNKS]
    shapes = [(h * GROUP + (META if p == len(homes) - 1 else 0), HEAD) for p, h in enumerate(homes)]
    whole = [pl.BlockSpec(s, lambda g: (0, 0)) for s in shapes]
    return pl.pallas_call(
        value_kernel,
        grid=(1,),
        in_specs=[
            pl.BlockSpec(got.shape, lambda g: (0, 0, 0)),
            pl.BlockSpec(weight.shape, lambda g: (0, 0, 0)),
        ],
        out_specs=whole,
        out_shape=[jax.ShapeDtypeStruct(s, BF16) for s in shapes],
        scratch_shapes=[pltpu.VMEM((VAL // LANES, max(homes) * GROUP, LANES), F32)],
        compiler_params=pltpu.CompilerParams(vmem_limit_bytes=24 * 2**20),
    )(got, weight)


def pack(rows):
    full = rows.shape[2] // LANES
    half = rows.shape[1] // 2
    tail = rows[:, :, full * LANES :]
    return [rows[:, :, t * LANES : (t + 1) * LANES] for t in range(full)] + [
        jnp.concatenate([tail[:, :half], tail[:, half:]], axis=2)
    ]


def unpack(packed, count):
    half = count // 2
    full = (packed.shape[0] - half) // count
    tail = packed[full * count :]
    tail = jnp.concatenate([tail[:, : LANES // 2], tail[:, LANES // 2 :]], axis=0)
    return jnp.concatenate([packed[t * count : (t + 1) * count] for t in range(full)] + [tail], axis=1)


def put(out, parts):
    at = 0
    for part in parts:
        out[:, at : at + part.shape[1], :] = part.astype(BF16)
        at += part.shape[1]


def fetch(order, blocks, held, sem):
    copies = [
        pltpu.make_async_copy(block, held.at[order[b]], sem.at[b])
        for b, block in enumerate(blocks)
    ]
    for copy in copies:
        copy.start()
    for copy in copies:
        copy.wait()


def multiply(held, home, weight):
    rows = jnp.concatenate(
        [held[:, h * home : (h + 1) * home, :].reshape(N * home, HEAD) for h in range(GROUP)], axis=1
    )
    rows = lax.dot_general(rows, weight[...], NT, preferred_element_type=F32)
    return rows.reshape(N, home, rows.shape[1]).astype(BF16)


def project_kernel(count, order, *refs):
    blocks, (weight, out, home_out, held, sem) = refs[:-5], refs[-5:]
    fetch(order, blocks, held, sem)
    rows = multiply(held, N * count * STEPS, weight)
    put(out, pack(rows.astype(F32)))
    home_out[...] = rows


def last_kernel(counts, order, *refs):
    parts = len(counts)
    refs, (weight, out, table_out, held, sem) = refs[:-5], refs[-5:]
    cut = len(refs) - (parts - 1)
    blocks, earlier = refs[:cut], refs[cut:]
    count = counts[-1]
    home = N * count * STEPS
    fetch(order, blocks, held, sem)
    table = held[:, GROUP * home :, :].astype(F32)
    table_out[...] = table
    table = table.astype(jnp.int32)
    rows = multiply(held, home, weight)
    cols = rows.shape[2]
    came = jnp.zeros((N * ARRIVING, cols), F32)
    for p, c in enumerate(counts):
        size = N * c * STEPS
        first = sum(counts[:p])
        lane = lax.broadcasted_iota(jnp.int32, (N, size), 1)
        taker = table[:, 2 * p, :size]
        slot = table[:, 2 * p + 1, :size]
        here = slot == first + (lane // STEPS) % c
        code = jnp.where(here, (taker * N + lane // (c * STEPS)) * STEPS + lane % STEPS, -1)
        source = rows if p == parts - 1 else earlier[p][...]
        group = max(1, 256 // size)
        for e in range(0, N, group):
            wanted = jnp.concatenate([code[e + g : e + g + 1] for g in range(group)], axis=1)
            r = lax.broadcasted_iota(jnp.int32, (N * ARRIVING, group * size), 0)
            pick = (r == wanted).astype(F32).astype(BF16)
            came = came + jnp.dot(
                pick, source[e : e + group].reshape(group * size, cols), preferred_element_type=F32
            )
    both = jnp.concatenate([rows.astype(F32), came.reshape(N, ARRIVING, cols)], axis=1)
    put(out, pack(both))


def project(counts, order, blocks, weight, earlier):
    cols, depth = weight.shape
    count = counts[-1]
    home = N * count * STEPS
    last = len(counts) == len(CHUNKS)
    sent = home + (ARRIVING if last else 0)
    earlier = earlier if last else []

    def kernel(*refs):
        if last:
            last_kernel(counts, *refs)
        else:
            project_kernel(count, *refs)

    def whole(shape):
        return pl.BlockSpec(shape, lambda g, *_: (0,) * len(shape))

    shapes = [(N, sent * cols // LANES, LANES), (N, META, LANES) if last else (N, home, cols)]
    return pl.pallas_call(
        kernel,
        grid_spec=pltpu.PrefetchScalarGridSpec(
            num_scalar_prefetch=1,
            grid=(1,),
            in_specs=[pl.BlockSpec(memory_space=pltpu.HBM)] * len(blocks)
            + [whole(e.shape) for e in earlier]
            + [whole(weight.shape)],
            out_specs=[whole(s) for s in shapes],
            scratch_shapes=[
                pltpu.VMEM((N,) + blocks[0].shape, BF16),
                pltpu.SemaphoreType.DMA((len(blocks),)),
            ],
        ),
        out_shape=[
            jax.ShapeDtypeStruct(shapes[0], BF16),
            jax.ShapeDtypeStruct(shapes[1], F32 if last else BF16),
        ],
        compiler_params=pltpu.CompilerParams(vmem_limit_bytes=48 * 2**20),
    )(order, *blocks, *earlier, weight)


def finish_kernel(mine, table, *refs):
    shares, out = refs[:-1], refs[-1]
    rows = []
    for got, (_, c) in zip(shares, CHUNKS, strict=True):
        total = got[0].astype(F32)
        for j in range(1, N):
            total = total + got[j].astype(F32)
        rows.append(unpack(total, total.shape[0] * LANES // out.shape[1]).astype(BF16))
    rows = jnp.concatenate(rows, axis=0)
    size = out.shape[0]
    o = lax.broadcasted_iota(jnp.int32, (size, size), 0)
    col = lax.broadcasted_iota(jnp.int32, (size, size), 1)
    slots = REQ + 1
    step, j, slot = o // (N * slots), (o // slots) % N, o % slots
    source = size - ARRIVING + j * STEPS + step
    before = 0
    for first, c in CHUNKS:
        inside = (slot >= first) & (slot < first + c)
        source = jnp.where(inside, before + j * c * STEPS + (slot - first) * STEPS + step, source)
        before += N * c * STEPS
    c0 = CHUNKS[0][1] * STEPS
    line = table[:, 1, : N * c0]
    row = lax.broadcasted_iota(jnp.int32, line.shape, 0)
    line = jnp.sum(jnp.where(row == mine[0], line, 0.0), axis=0, keepdims=True)
    r = lax.broadcasted_iota(jnp.int32, (size, N * c0), 0)
    lane = lax.broadcasted_iota(jnp.int32, (size, N * c0), 1)
    pick_slot = ((r // slots) % N) * c0 == lane
    away = jnp.sum(jnp.where(pick_slot, line, 0.0), axis=1, keepdims=True)
    slot_of = lax.broadcasted_iota(jnp.int32, (size, 1), 0) % slots
    stays = (slot_of == REQ) | (slot_of.astype(F32) != away)
    pick = ((col == source) & stays).astype(F32).astype(BF16)
    out[...] = jnp.dot(pick, rows, preferred_element_type=F32).astype(BF16)


def finish(mine, table, shares, cols):
    vmem = pl.BlockSpec(memory_space=pltpu.VMEM)
    size = sum(s.shape[1] for s in shares) * LANES // cols
    return pl.pallas_call(
        finish_kernel,
        in_specs=[pl.BlockSpec(memory_space=pltpu.SMEM), vmem] + [vmem] * len(shares),
        out_specs=vmem,
        out_shape=jax.ShapeDtypeStruct((size, cols), BF16),
        compiler_params=pltpu.CompilerParams(vmem_limit_bytes=16 * 2**20),
    )(mine, table, *shares)


def along_z(by):
    chips = N // 2
    return [(z * 2 + c, (z + by) % chips * 2 + c) for z in range(chips) for c in range(2)]


OTHER_CORE = [(i, i ^ 1) for i in range(N)]


def gather(block):
    me = lax.axis_index("dp")
    chips = N // 2
    held = [(block, me)]
    up = down = block
    for hop in range(1, chips // 2 + 1):
        up = lax.ppermute(up, "dp", along_z(1))
        held.append((up, (me + N - 2 * hop) % N))
        if hop < chips // 2:
            down = lax.ppermute(down, "dp", along_z(-1))
            held.append((down, (me + 2 * hop) % N))
    held += [(lax.ppermute(b, "dp", OTHER_CORE), i ^ 1) for b, i in held]
    return [b for b, _ in held], jnp.stack([i for _, i in held]).astype(jnp.int32)


def across_tp(x):
    return lax.all_to_all(x, "tp", split_axis=0, concat_axis=0, tiled=True)


def shards(latent_cache, lengths, queries, new_latents, migrations, value_weight, output_weight):
    cache = jnp.swapaxes(latent_cache, 1, 2)
    asked = jnp.swapaxes(queries, 2, 3)
    weight = jnp.swapaxes(output_weight, 0, 1)
    counts = tuple(c for _, c in CHUNKS)
    sent = attend(lengths, migrations, asked, cache, new_latents)
    hidden = values(across_tp(sent), value_weight)
    blocks, order = gather(hidden[0])
    partial, table = project(counts, order, blocks, weight, [])
    shares = across_tp(partial)
    mine = lax.axis_index("tp").astype(jnp.int32).reshape(1)
    return finish(mine, table, [shares], weight.shape[0])


def solution(mesh):
    return jax.shard_map(
        shards,
        mesh=mesh,
        in_specs=(
            P(("dp", "tp"), None, None),
            P(("dp", "tp")),
            P(None, ("dp", "tp"), None, None),
            P(None, ("dp", "tp"), None),
            P(("dp", "tp"), None),
            P("tp", None, None),
            P("tp", "dp"),
        ),
        out_specs=P("tp", "dp"),
        check_vma=False,
    )
```

```python
import math

import jax
import jax.numpy as jnp
from jax import lax
from jax.experimental import pallas as pl
from jax.experimental.pallas import tpu as pltpu
from jax.sharding import PartitionSpec as P

NOPE = 128
ROPE = 64
VAL = 512
HEAD = 128
REQ = 4
STEPS = 2
N = 16
GROUP = 8
META = 16
LANES = 128
CHUNKS = ((0, 4),)
ARRIVING = N * STEPS
TOGETHER = 2
F32 = jnp.float32
BF16 = jnp.bfloat16
SCALE = 1.0 / math.sqrt(NOPE + ROPE) * math.log2(math.e)
NT = (((1,), (1,)), ((), ()))


def attend_one(q, keys, own, filled):
    far = jnp.dot(q, keys, preferred_element_type=F32)
    near = lax.dot_general(q, own, NT, preferred_element_type=F32)
    far_ok = lax.broadcasted_iota(jnp.int32, (1, keys.shape[1]), 1) < filled
    step = lax.broadcasted_iota(jnp.int32, near.shape, 0) // (N * GROUP)
    near_ok = lax.broadcasted_iota(jnp.int32, near.shape, 1) <= step
    far = jnp.where(far_ok, far, -jnp.inf)
    near = jnp.where(near_ok, near, -jnp.inf)
    top = jnp.maximum(jnp.max(far, axis=1, keepdims=True), jnp.max(near, axis=1, keepdims=True))
    far = jnp.exp2((far - top) * SCALE)
    near = jnp.exp2((near - top) * SCALE)
    total = jnp.sum(far, axis=1, keepdims=True) + jnp.sum(near, axis=1, keepdims=True)
    mixed = lax.dot_general(far.astype(BF16), keys[:VAL], NT, preferred_element_type=F32)
    mixed = mixed + jnp.dot(near.astype(BF16), own[:, :VAL], preferred_element_type=F32)
    return mixed * (1.0 / total)


def attend_kernel(lengths, moves, query, cache, new, out):
    half = N * GROUP
    rows = STEPS * GROUP
    body = REQ * rows
    turn = pl.program_id(0)
    for u in range(TOGETHER):
        request = turn * TOGETHER + u
        q = jnp.concatenate([query[s, u].T for s in range(STEPS)], axis=0)
        fresh = new[...].astype(F32)
        fresh = jnp.where(turn == 0, fresh[:, u, :], fresh[:, TOGETHER + u, :])
        own = jnp.concatenate([fresh, jnp.zeros((META - STEPS, fresh.shape[1]), F32)], axis=0)
        mixed = attend_one(q, cache[u], own.astype(BF16), lengths[request])
        mixed = jnp.concatenate(
            [mixed[:half].reshape(N, GROUP, VAL), mixed[half:].reshape(N, GROUP, VAL)], axis=1
        ).astype(BF16)
        for p in range(VAL // LANES):
            at = pl.multiple_of(p * body + request * rows, rows)
            out[:, pl.ds(at, rows), :] = mixed[:, :, p * LANES : (p + 1) * LANES]
    lane = lax.broadcasted_iota(jnp.int32, (N, META, LANES), 2)
    slot = moves[0, 0]
    taker = jnp.where(slot < REQ, moves[0, 1], -1)
    out[:, body * (VAL // LANES) :, :] = (
        jnp.where(lane < LANES // 2, taker, slot).astype(F32).astype(BF16)
    )


def attend(lengths, moves, queries, cache, new):
    width = cache.shape[1]
    rows = REQ * STEPS * GROUP * (VAL // LANES) + META
    return pl.pallas_call(
        attend_kernel,
        grid_spec=pltpu.PrefetchScalarGridSpec(
            num_scalar_prefetch=2,
            grid=(REQ // TOGETHER,),
            in_specs=[
                pl.BlockSpec((STEPS, TOGETHER, width, N * GROUP), lambda g, *_: (0, g, 0, 0)),
                pl.BlockSpec((TOGETHER, width, cache.shape[2]), lambda g, *_: (g, 0, 0)),
                pl.BlockSpec(new.shape, lambda g, *_: (0, 0, 0)),
            ],
            out_specs=pl.BlockSpec((N, rows, LANES), lambda g, *_: (0, 0, 0)),
        ),
        out_shape=jax.ShapeDtypeStruct((N, rows, LANES), BF16),
        compiler_params=pltpu.CompilerParams(vmem_limit_bytes=56 * 2**20),
    )(lengths, moves, queries, cache, new)


def value_kernel(got, weight, *refs):
    outs, wide = refs[:-1], refs[-1]
    body = REQ * STEPS * GROUP
    pieces = VAL // LANES
    moves = got[:, pieces * body :, :].astype(F32)[:, 0, :]
    sub = lax.broadcasted_iota(jnp.int32, (N, LANES), 0)
    lane = lax.broadcasted_iota(jnp.int32, (N, LANES), 1)
    taker = jnp.max(jnp.where(lane < LANES // 2, moves, -1.0), axis=1, keepdims=True)
    slot = jnp.max(jnp.where(lane < LANES // 2, -1.0, moves), axis=1, keepdims=True)
    parts = []
    for (first, count), out in zip(CHUNKS, outs, strict=True):
        cell = count * STEPS * GROUP
        home = N * count * STEPS
        for p in range(pieces):
            at = p * body + first * STEPS * GROUP
            wide[p, : N * cell, :] = got[:, at : at + cell, :].astype(F32).reshape(N * cell, LANES)
        for h in range(GROUP):
            rows = jnp.concatenate(
                [wide[p, pl.ds(h, home, stride=GROUP), :] for p in range(pieces)], axis=1
            ).astype(BF16)
            out[h * home : (h + 1) * home, :] = jnp.dot(
                rows, weight[h], preferred_element_type=F32
            ).astype(BF16)
        mine = lane // (count * STEPS) == sub
        for v in (taker, slot):
            parts.append(jnp.sum(jnp.where(mine, v, 0.0), axis=0, keepdims=True))
    row = lax.broadcasted_iota(jnp.int32, (META, LANES), 0)
    lines = jnp.zeros((META, LANES), F32)
    for i, part in enumerate(parts):
        lines = jnp.where(row == i, part, lines)
    out[GROUP * home :, :] = lines.astype(BF16)


def values(got, weight):
    homes = [N * count * STEPS for _, count in CHUNKS]
    shapes = [(h * GROUP + (META if p == len(homes) - 1 else 0), HEAD) for p, h in enumerate(homes)]
    whole = [pl.BlockSpec(s, lambda g: (0, 0)) for s in shapes]
    return pl.pallas_call(
        value_kernel,
        grid=(1,),
        in_specs=[
            pl.BlockSpec(got.shape, lambda g: (0, 0, 0)),
            pl.BlockSpec(weight.shape, lambda g: (0, 0, 0)),
        ],
        out_specs=whole,
        out_shape=[jax.ShapeDtypeStruct(s, BF16) for s in shapes],
        scratch_shapes=[pltpu.VMEM((VAL // LANES, max(homes) * GROUP, LANES), F32)],
        compiler_params=pltpu.CompilerParams(vmem_limit_bytes=24 * 2**20),
    )(got, weight)


def pack(rows):
    full = rows.shape[2] // LANES
    half = rows.shape[1] // 2
    tail = rows[:, :, full * LANES :]
    return [rows[:, :, t * LANES : (t + 1) * LANES] for t in range(full)] + [
        jnp.concatenate([tail[:, :half], tail[:, half:]], axis=2)
    ]


def unpack(packed, count):
    half = count // 2
    full = (packed.shape[0] - half) // count
    tail = packed[full * count :]
    tail = jnp.concatenate([tail[:, : LANES // 2], tail[:, LANES // 2 :]], axis=0)
    return jnp.concatenate([packed[t * count : (t + 1) * count] for t in range(full)] + [tail], axis=1)


def put(out, parts):
    at = 0
    for part in parts:
        out[:, at : at + part.shape[1], :] = part.astype(BF16)
        at += part.shape[1]


def fetch(order, blocks, held, sem):
    copies = [
        pltpu.make_async_copy(block, held.at[order[b]], sem.at[b])
        for b, block in enumerate(blocks)
    ]
    for copy in copies:
        copy.start()
    for copy in copies:
        copy.wait()


def multiply(held, home, weight):
    rows = jnp.concatenate(
        [held[:, h * home : (h + 1) * home, :].reshape(N * home, HEAD) for h in range(GROUP)], axis=1
    )
    rows = lax.dot_general(rows, weight[...], NT, preferred_element_type=F32)
    return rows.reshape(N, home, rows.shape[1]).astype(BF16)


def project_kernel(count, order, *refs):
    blocks, (weight, out, home_out, held, sem) = refs[:-5], refs[-5:]
    fetch(order, blocks, held, sem)
    rows = multiply(held, N * count * STEPS, weight)
    put(out, pack(rows.astype(F32)))
    home_out[...] = rows


def last_kernel(counts, order, *refs):
    parts = len(counts)
    refs, (weight, out, table_out, held, sem) = refs[:-5], refs[-5:]
    cut = len(refs) - (parts - 1)
    blocks, earlier = refs[:cut], refs[cut:]
    count = counts[-1]
    home = N * count * STEPS
    fetch(order, blocks, held, sem)
    table = held[:, GROUP * home :, :].astype(F32)
    table_out[...] = table
    table = table.astype(jnp.int32)
    rows = multiply(held, home, weight)
    cols = rows.shape[2]
    came = jnp.zeros((N * ARRIVING, cols), F32)
    for p, c in enumerate(counts):
        size = N * c * STEPS
        first = sum(counts[:p])
        lane = lax.broadcasted_iota(jnp.int32, (N, size), 1)
        taker = table[:, 2 * p, :size]
        slot = table[:, 2 * p + 1, :size]
        here = slot == first + (lane // STEPS) % c
        code = jnp.where(here, (taker * N + lane // (c * STEPS)) * STEPS + lane % STEPS, -1)
        source = rows if p == parts - 1 else earlier[p][...]
        group = max(1, 256 // size)
        for e in range(0, N, group):
            wanted = jnp.concatenate([code[e + g : e + g + 1] for g in range(group)], axis=1)
            r = lax.broadcasted_iota(jnp.int32, (N * ARRIVING, group * size), 0)
            pick = (r == wanted).astype(F32).astype(BF16)
            came = came + jnp.dot(
                pick, source[e : e + group].reshape(group * size, cols), preferred_element_type=F32
            )
    both = jnp.concatenate([rows.astype(F32), came.reshape(N, ARRIVING, cols)], axis=1)
    put(out, pack(both))


def project(counts, order, blocks, weight, earlier):
    cols, depth = weight.shape
    count = counts[-1]
    home = N * count * STEPS
    last = len(counts) == len(CHUNKS)
    sent = home + (ARRIVING if last else 0)
    earlier = earlier if last else []

    def kernel(*refs):
        if last:
            last_kernel(counts, *refs)
        else:
            project_kernel(count, *refs)

    def whole(shape):
        return pl.BlockSpec(shape, lambda g, *_: (0,) * len(shape))

    shapes = [(N, sent * cols // LANES, LANES), (N, META, LANES) if last else (N, home, cols)]
    return pl.pallas_call(
        kernel,
        grid_spec=pltpu.PrefetchScalarGridSpec(
            num_scalar_prefetch=1,
            grid=(1,),
            in_specs=[pl.BlockSpec(memory_space=pltpu.HBM)] * len(blocks)
            + [whole(e.shape) for e in earlier]
            + [whole(weight.shape)],
            out_specs=[whole(s) for s in shapes],
            scratch_shapes=[
                pltpu.VMEM((N,) + blocks[0].shape, BF16),
                pltpu.SemaphoreType.DMA((len(blocks),)),
            ],
        ),
        out_shape=[
            jax.ShapeDtypeStruct(shapes[0], BF16),
            jax.ShapeDtypeStruct(shapes[1], F32 if last else BF16),
        ],
        compiler_params=pltpu.CompilerParams(vmem_limit_bytes=48 * 2**20),
    )(order, *blocks, *earlier, weight)


def finish_kernel(mine, table, *refs):
    shares, out = refs[:-1], refs[-1]
    rows = []
    for got, (_, c) in zip(shares, CHUNKS, strict=True):
        total = got[0].astype(F32)
        for j in range(1, N):
            total = total + got[j].astype(F32)
        rows.append(unpack(total, total.shape[0] * LANES // out.shape[1]).astype(BF16))
    rows = jnp.concatenate(rows, axis=0)
    size = out.shape[0]
    o = lax.broadcasted_iota(jnp.int32, (size, size), 0)
    col = lax.broadcasted_iota(jnp.int32, (size, size), 1)
    slots = REQ + 1
    step, j, slot = o // (N * slots), (o // slots) % N, o % slots
    source = size - ARRIVING + j * STEPS + step
    before = 0
    for first, c in CHUNKS:
        inside = (slot >= first) & (slot < first + c)
        source = jnp.where(inside, before + j * c * STEPS + (slot - first) * STEPS + step, source)
        before += N * c * STEPS
    c0 = CHUNKS[0][1] * STEPS
    line = table[:, 1, : N * c0]
    row = lax.broadcasted_iota(jnp.int32, line.shape, 0)
    line = jnp.sum(jnp.where(row == mine[0], line, 0.0), axis=0, keepdims=True)
    r = lax.broadcasted_iota(jnp.int32, (size, N * c0), 0)
    lane = lax.broadcasted_iota(jnp.int32, (size, N * c0), 1)
    pick_slot = ((r // slots) % N) * c0 == lane
    away = jnp.sum(jnp.where(pick_slot, line, 0.0), axis=1, keepdims=True)
    slot_of = lax.broadcasted_iota(jnp.int32, (size, 1), 0) % slots
    stays = (slot_of == REQ) | (slot_of.astype(F32) != away)
    pick = ((col == source) & stays).astype(F32).astype(BF16)
    out[...] = jnp.dot(pick, rows, preferred_element_type=F32).astype(BF16)


def finish(mine, table, shares, cols):
    vmem = pl.BlockSpec(memory_space=pltpu.VMEM)
    size = sum(s.shape[1] for s in shares) * LANES // cols
    return pl.pallas_call(
        finish_kernel,
        in_specs=[pl.BlockSpec(memory_space=pltpu.SMEM), vmem] + [vmem] * len(shares),
        out_specs=vmem,
        out_shape=jax.ShapeDtypeStruct((size, cols), BF16),
        compiler_params=pltpu.CompilerParams(vmem_limit_bytes=16 * 2**20),
    )(mine, table, *shares)


def along_z(by):
    chips = N // 2
    return [(z * 2 + c, (z + by) % chips * 2 + c) for z in range(chips) for c in range(2)]


OTHER_CORE = [(i, i ^ 1) for i in range(N)]


def gather(block):
    me = lax.axis_index("dp")
    chips = N // 2
    held = [(block, me)]
    up = down = block
    for hop in range(1, chips // 2 + 1):
        up = lax.ppermute(up, "dp", along_z(1))
        held.append((up, (me + N - 2 * hop) % N))
        if hop < chips // 2:
            down = lax.ppermute(down, "dp", along_z(-1))
            held.append((down, (me + 2 * hop) % N))
    held += [(lax.ppermute(b, "dp", OTHER_CORE), i ^ 1) for b, i in held]
    return [b for b, _ in held], jnp.stack([i for _, i in held]).astype(jnp.int32)


def across_tp(x):
    return lax.all_to_all(x, "tp", split_axis=0, concat_axis=0, tiled=True)


def shards(latent_cache, lengths, queries, new_latents, migrations, value_weight, output_weight):
    cache = jnp.swapaxes(latent_cache, 1, 2)
    asked = jnp.swapaxes(queries, 2, 3)
    weight = jnp.swapaxes(output_weight, 0, 1)
    counts = tuple(c for _, c in CHUNKS)
    sent = attend(lengths, migrations, asked, cache, new_latents)
    hidden = values(across_tp(sent), value_weight)
    blocks, order = gather(hidden[0])
    partial, table = project(counts, order, blocks, weight, [])
    mine = lax.axis_index("tp").astype(jnp.int32).reshape(1)
    partial, table, mine = lax.optimization_barrier((partial, table, mine))
    shares = across_tp(partial)
    return finish(mine, table, [shares], weight.shape[0])


def solution(mesh):
    return jax.shard_map(
        shards,
        mesh=mesh,
        in_specs=(
            P(("dp", "tp"), None, None),
            P(("dp", "tp")),
            P(None, ("dp", "tp"), None, None),
            P(None, ("dp", "tp"), None),
            P(("dp", "tp"), None),
            P("tp", None, None),
            P("tp", "dp"),
        ),
        out_specs=P("tp", "dp"),
        check_vma=False,
    )
```

```python
import math

import jax
import jax.numpy as jnp
from jax import lax
from jax.experimental import pallas as pl
from jax.experimental.pallas import tpu as pltpu
from jax.sharding import PartitionSpec as P

NOPE = 128
ROPE = 64
VAL = 512
HEAD = 128
REQ = 4
STEPS = 2
N = 16
GROUP = 8
META = 16
LANES = 128
CHUNKS = ((0, 4),)
CELL = REQ * STEPS
HOME = N * CELL
AT_ONCE = 8
ARRIVING = N * STEPS
TOGETHER = 2
F32 = jnp.float32
BF16 = jnp.bfloat16
SCALE = 1.0 / math.sqrt(NOPE + ROPE) * math.log2(math.e)
NT = (((1,), (1,)), ((), ()))


def attend_one(q, keys, own, filled):
    far = jnp.dot(q, keys, preferred_element_type=F32)
    near = lax.dot_general(q, own, NT, preferred_element_type=F32)
    far_ok = lax.broadcasted_iota(jnp.int32, (1, keys.shape[1]), 1) < filled
    step = lax.broadcasted_iota(jnp.int32, near.shape, 0) // (N * GROUP)
    near_ok = lax.broadcasted_iota(jnp.int32, near.shape, 1) <= step
    far = jnp.where(far_ok, far, -jnp.inf)
    near = jnp.where(near_ok, near, -jnp.inf)
    top = jnp.maximum(jnp.max(far, axis=1, keepdims=True), jnp.max(near, axis=1, keepdims=True))
    far = jnp.exp2((far - top) * SCALE)
    near = jnp.exp2((near - top) * SCALE)
    total = jnp.sum(far, axis=1, keepdims=True) + jnp.sum(near, axis=1, keepdims=True)
    mixed = lax.dot_general(far.astype(BF16), keys[:VAL], NT, preferred_element_type=F32)
    mixed = mixed + jnp.dot(near.astype(BF16), own[:, :VAL], preferred_element_type=F32)
    return mixed * (1.0 / total)


def attend_kernel(lengths, moves, query, cache, new, out):
    half = N * GROUP
    rows = STEPS * GROUP
    body = REQ * rows
    turn = pl.program_id(0)
    for u in range(TOGETHER):
        request = turn * TOGETHER + u
        q = jnp.concatenate([query[s, u].T for s in range(STEPS)], axis=0)
        fresh = new[...].astype(F32)
        fresh = jnp.where(turn == 0, fresh[:, u, :], fresh[:, TOGETHER + u, :])
        own = jnp.concatenate([fresh, jnp.zeros((META - STEPS, fresh.shape[1]), F32)], axis=0)
        mixed = attend_one(q, cache[u], own.astype(BF16), lengths[request])
        mixed = jnp.concatenate(
            [mixed[:half].reshape(N, GROUP, VAL), mixed[half:].reshape(N, GROUP, VAL)], axis=1
        ).astype(BF16)
        for p in range(VAL // LANES):
            at = pl.multiple_of(p * body + request * rows, rows)
            out[:, pl.ds(at, rows), :] = mixed[:, :, p * LANES : (p + 1) * LANES]
    lane = lax.broadcasted_iota(jnp.int32, (N, META, LANES), 2)
    slot = moves[0, 0]
    taker = jnp.where(slot < REQ, moves[0, 1], -1)
    out[:, body * (VAL // LANES) :, :] = (
        jnp.where(lane < LANES // 2, taker, slot).astype(F32).astype(BF16)
    )


def attend(lengths, moves, queries, cache, new):
    width = cache.shape[1]
    rows = REQ * STEPS * GROUP * (VAL // LANES) + META
    return pl.pallas_call(
        attend_kernel,
        grid_spec=pltpu.PrefetchScalarGridSpec(
            num_scalar_prefetch=2,
            grid=(REQ // TOGETHER,),
            in_specs=[
                pl.BlockSpec((STEPS, TOGETHER, width, N * GROUP), lambda g, *_: (0, g, 0, 0)),
                pl.BlockSpec((TOGETHER, width, cache.shape[2]), lambda g, *_: (g, 0, 0)),
                pl.BlockSpec(new.shape, lambda g, *_: (0, 0, 0)),
            ],
            out_specs=pl.BlockSpec((N, rows, LANES), lambda g, *_: (0, 0, 0)),
        ),
        out_shape=jax.ShapeDtypeStruct((N, rows, LANES), BF16),
        compiler_params=pltpu.CompilerParams(vmem_limit_bytes=56 * 2**20),
    )(lengths, moves, queries, cache, new)


def value_kernel(got, weight, *refs):
    outs, wide = refs[:-1], refs[-1]
    body = REQ * STEPS * GROUP
    pieces = VAL // LANES
    moves = got[:, pieces * body :, :].astype(F32)[:, 0, :]
    sub = lax.broadcasted_iota(jnp.int32, (N, LANES), 0)
    lane = lax.broadcasted_iota(jnp.int32, (N, LANES), 1)
    taker = jnp.max(jnp.where(lane < LANES // 2, moves, -1.0), axis=1, keepdims=True)
    slot = jnp.max(jnp.where(lane < LANES // 2, -1.0, moves), axis=1, keepdims=True)
    parts = []
    for (first, count), out in zip(CHUNKS, outs, strict=True):
        cell = count * STEPS * GROUP
        home = N * count * STEPS
        for p in range(pieces):
            at = p * body + first * STEPS * GROUP
            wide[p, : N * cell, :] = got[:, at : at + cell, :].astype(F32).reshape(N * cell, LANES)
        for h in range(GROUP):
            rows = jnp.concatenate(
                [wide[p, pl.ds(h, home, stride=GROUP), :] for p in range(pieces)], axis=1
            ).astype(BF16)
            out[h * home : (h + 1) * home, :] = jnp.dot(
                rows, weight[h], preferred_element_type=F32
            ).astype(BF16)
        mine = lane // (count * STEPS) == sub
        for v in (taker, slot):
            parts.append(jnp.sum(jnp.where(mine, v, 0.0), axis=0, keepdims=True))
    row = lax.broadcasted_iota(jnp.int32, (META, LANES), 0)
    lines = jnp.zeros((META, LANES), F32)
    for i, part in enumerate(parts):
        lines = jnp.where(row == i, part, lines)
    out[GROUP * home :, :] = lines.astype(BF16)


def values(got, weight):
    homes = [N * count * STEPS for _, count in CHUNKS]
    shapes = [(h * GROUP + (META if p == len(homes) - 1 else 0), HEAD) for p, h in enumerate(homes)]
    whole = [pl.BlockSpec(s, lambda g: (0, 0)) for s in shapes]
    return pl.pallas_call(
        value_kernel,
        grid=(1,),
        in_specs=[
            pl.BlockSpec(got.shape, lambda g: (0, 0, 0)),
            pl.BlockSpec(weight.shape, lambda g: (0, 0, 0)),
        ],
        out_specs=whole,
        out_shape=[jax.ShapeDtypeStruct(s, BF16) for s in shapes],
        scratch_shapes=[pltpu.VMEM((VAL // LANES, max(homes) * GROUP, LANES), F32)],
        compiler_params=pltpu.CompilerParams(vmem_limit_bytes=24 * 2**20),
    )(got, weight)


def pack(rows):
    full = rows.shape[2] // LANES
    half = rows.shape[1] // 2
    tail = rows[:, :, full * LANES :]
    return [rows[:, :, t * LANES : (t + 1) * LANES] for t in range(full)] + [
        jnp.concatenate([tail[:, :half], tail[:, half:]], axis=2)
    ]


def unpack(packed, count):
    half = count // 2
    full = (packed.shape[0] - half) // count
    tail = packed[full * count :]
    tail = jnp.concatenate([tail[:, : LANES // 2], tail[:, LANES // 2 :]], axis=0)
    return jnp.concatenate([packed[t * count : (t + 1) * count] for t in range(full)] + [tail], axis=1)


def put(out, parts):
    at = 0
    for part in parts:
        out[:, at : at + part.shape[1], :] = part.astype(BF16)
        at += part.shape[1]


def project_kernel(order, *refs):
    blocks, (weight, out, table_out, held, taps, staged, extra, sem) = refs[:N], refs[N:]
    fill = pltpu.make_async_copy(weight, taps, sem.at[2 * N])
    fill.start()
    copies = [
        pltpu.make_async_copy(block, held.at[b], sem.at[b]) for b, block in enumerate(blocks)
    ]
    for copy in copies:
        copy.start()
    fill.wait()
    cols = taps.shape[0]
    size = staged.shape[1]
    lane = lax.broadcasted_iota(jnp.int32, (1, HOME), 1)
    sub = lax.broadcasted_iota(jnp.int32, (N, HOME), 0)
    table = jnp.zeros((N, HOME), F32)
    sends, halves, codes = [], [], []
    for first in range(0, N, AT_ONCE):
        for copy in copies[first : first + AT_ONCE]:
            copy.wait()
        depth = [
            held[first : first + AT_ONCE, h * HOME : (h + 1) * HOME, :].reshape(AT_ONCE * HOME, HEAD)
            for h in range(GROUP)
        ]
        rows = lax.dot_general(
            jnp.concatenate(depth, axis=1), taps[...], NT, preferred_element_type=F32
        )
        at = 0
        for part in pack(rows.reshape(AT_ONCE, HOME, cols)):
            staged[first : first + AT_ONCE, at : at + part.shape[1], :] = part.astype(BF16)
            at += part.shape[1]
        for b in range(first, first + AT_ONCE):
            send = pltpu.make_async_copy(
                staged.at[b], out.at[order[b], pl.ds(0, size)], sem.at[N + b]
            )
            send.start()
            sends.append(send)
            line = held[b, GROUP * HOME :, :].astype(F32)
            table = jnp.where(sub == order[b], line[1:2], table)
            line = line.astype(jnp.int32)
            here = line[1:2] == (lane % CELL) // STEPS
            codes.append(jnp.where(here, (line[0:1] * N + lane // CELL) * STEPS + lane % STEPS, -1))
        halves.append(rows.astype(BF16))
    table_out[...] = table
    came = jnp.zeros((N * ARRIVING, cols), F32)
    for g, rows in enumerate(halves):
        wanted = jnp.concatenate(codes[g * AT_ONCE : (g + 1) * AT_ONCE], axis=1)
        r = lax.broadcasted_iota(jnp.int32, (N * ARRIVING, wanted.shape[1]), 0)
        pick = (r == wanted).astype(F32).astype(BF16)
        came = came + jnp.dot(pick, rows, preferred_element_type=F32)
    at = 0
    for part in pack(came.reshape(N, ARRIVING, cols)):
        extra[:, at : at + part.shape[1], :] = part.astype(BF16)
        at += part.shape[1]
    rest = pltpu.make_async_copy(extra, out.at[:, pl.ds(size, extra.shape[1])], sem.at[2 * N + 1])
    rest.start()
    sends.append(rest)
    for send in sends:
        send.wait()


def project(order, blocks, weight):
    cols = weight.shape[0]
    packed = HOME * cols // LANES
    added = ARRIVING * cols // LANES
    hbm = pl.BlockSpec(memory_space=pltpu.HBM)
    return pl.pallas_call(
        project_kernel,
        grid_spec=pltpu.PrefetchScalarGridSpec(
            num_scalar_prefetch=1,
            grid=(1,),
            in_specs=[hbm] * (N + 1),
            out_specs=[hbm, pl.BlockSpec((N, HOME), lambda g, *_: (0, 0))],
            scratch_shapes=[
                pltpu.VMEM((N,) + blocks[0].shape, BF16),
                pltpu.VMEM(weight.shape, BF16),
                pltpu.VMEM((N, packed, LANES), BF16),
                pltpu.VMEM((N, added, LANES), BF16),
                pltpu.SemaphoreType.DMA((2 * N + 2,)),
            ],
        ),
        out_shape=[
            jax.ShapeDtypeStruct((N, packed + added, LANES), BF16),
            jax.ShapeDtypeStruct((N, HOME), F32),
        ],
        compiler_params=pltpu.CompilerParams(vmem_limit_bytes=50 * 2**20),
    )(order, *blocks, weight)


def finish_kernel(mine, table, got, out):
    total = got[0].astype(F32)
    for j in range(1, N):
        total = total + got[j].astype(F32)
    size, cols = out.shape
    packed = HOME * cols // LANES
    rows = jnp.concatenate(
        [unpack(total[:packed], HOME), unpack(total[packed:], ARRIVING)], axis=0
    ).astype(BF16)
    o = lax.broadcasted_iota(jnp.int32, (size, size), 0)
    col = lax.broadcasted_iota(jnp.int32, (size, size), 1)
    slots = REQ + 1
    step, j, slot = o // (N * slots), (o // slots) % N, o % slots
    source = jnp.where(slot < REQ, j * CELL + slot * STEPS + step, HOME + j * STEPS + step)
    line = table[...]
    row = lax.broadcasted_iota(jnp.int32, line.shape, 0)
    line = jnp.sum(jnp.where(row == mine[0], line, 0.0), axis=0, keepdims=True)
    r = lax.broadcasted_iota(jnp.int32, (size, HOME), 0)
    lane = lax.broadcasted_iota(jnp.int32, (size, HOME), 1)
    pick_slot = ((r // slots) % N) * CELL == lane
    away = jnp.sum(jnp.where(pick_slot, line, 0.0), axis=1, keepdims=True)
    slot_of = lax.broadcasted_iota(jnp.int32, (size, 1), 0) % slots
    stays = (slot_of == REQ) | (slot_of.astype(F32) != away)
    pick = ((col == source) & stays).astype(F32).astype(BF16)
    out[...] = jnp.dot(pick, rows, preferred_element_type=F32).astype(BF16)


def finish(mine, table, got, cols):
    vmem = pl.BlockSpec(memory_space=pltpu.VMEM)
    return pl.pallas_call(
        finish_kernel,
        in_specs=[pl.BlockSpec(memory_space=pltpu.SMEM), vmem, vmem],
        out_specs=vmem,
        out_shape=jax.ShapeDtypeStruct((HOME + ARRIVING, cols), BF16),
        compiler_params=pltpu.CompilerParams(vmem_limit_bytes=16 * 2**20),
    )(mine, table, got)


def along_z(by):
    chips = N // 2
    return [(z * 2 + c, (z + by) % chips * 2 + c) for z in range(chips) for c in range(2)]


OTHER_CORE = [(i, i ^ 1) for i in range(N)]


def gather(block):
    me = lax.axis_index("dp")
    chips = N // 2
    held = [(block, me)]
    up = down = block
    for hop in range(1, chips // 2 + 1):
        up = lax.ppermute(up, "dp", along_z(1))
        held.append((up, (me + N - 2 * hop) % N))
        if hop < chips // 2:
            down = lax.ppermute(down, "dp", along_z(-1))
            held.append((down, (me + 2 * hop) % N))
    held += [(lax.ppermute(b, "dp", OTHER_CORE), i ^ 1) for b, i in held]
    return [b for b, _ in held], jnp.stack([i for _, i in held]).astype(jnp.int32)


def across_tp(x):
    return lax.all_to_all(x, "tp", split_axis=0, concat_axis=0, tiled=True)


def shards(latent_cache, lengths, queries, new_latents, migrations, value_weight, output_weight):
    cache = jnp.swapaxes(latent_cache, 1, 2)
    asked = jnp.swapaxes(queries, 2, 3)
    weight = jnp.swapaxes(output_weight, 0, 1)
    sent = attend(lengths, migrations, asked, cache, new_latents)
    hidden = values(across_tp(sent), value_weight)
    blocks, order = gather(hidden[0])
    partial, table = project(order, blocks, weight)
    mine = lax.axis_index("tp").astype(jnp.int32).reshape(1)
    partial, table, mine = lax.optimization_barrier((partial, table, mine))
    shares = across_tp(partial)
    return finish(mine, table, shares, weight.shape[0])


def solution(mesh):
    return jax.shard_map(
        shards,
        mesh=mesh,
        in_specs=(
            P(("dp", "tp"), None, None),
            P(("dp", "tp")),
            P(None, ("dp", "tp"), None, None),
            P(None, ("dp", "tp"), None),
            P(("dp", "tp"), None),
            P("tp", None, None),
            P("tp", "dp"),
        ),
        out_specs=P("tp", "dp"),
        check_vma=False,
    )
```

```python
import math

import jax
import jax.numpy as jnp
from jax import lax
from jax.experimental import pallas as pl
from jax.experimental.pallas import tpu as pltpu
from jax.sharding import PartitionSpec as P

NOPE = 128
ROPE = 64
VAL = 512
HEAD = 128
REQ = 4
STEPS = 2
N = 16
GROUP = 8
META = 16
LANES = 128
CHUNKS = ((0, 4),)
CELL = REQ * STEPS
HOME = N * CELL
AT_ONCE = 16
ARRIVING = N * STEPS
TOGETHER = 2
F32 = jnp.float32
BF16 = jnp.bfloat16
SCALE = 1.0 / math.sqrt(NOPE + ROPE) * math.log2(math.e)
NT = (((1,), (1,)), ((), ()))


def attend_one(q, keys, own, filled):
    far = jnp.dot(q, keys, preferred_element_type=F32)
    near = lax.dot_general(q, own, NT, preferred_element_type=F32)
    far_ok = lax.broadcasted_iota(jnp.int32, (1, keys.shape[1]), 1) < filled
    step = lax.broadcasted_iota(jnp.int32, near.shape, 0) // (N * GROUP)
    near_ok = lax.broadcasted_iota(jnp.int32, near.shape, 1) <= step
    far = jnp.where(far_ok, far, -jnp.inf)
    near = jnp.where(near_ok, near, -jnp.inf)
    top = jnp.maximum(jnp.max(far, axis=1, keepdims=True), jnp.max(near, axis=1, keepdims=True))
    far = jnp.exp2((far - top) * SCALE)
    near = jnp.exp2((near - top) * SCALE)
    total = jnp.sum(far, axis=1, keepdims=True) + jnp.sum(near, axis=1, keepdims=True)
    mixed = lax.dot_general(far.astype(BF16), keys[:VAL], NT, preferred_element_type=F32)
    mixed = mixed + jnp.dot(near.astype(BF16), own[:, :VAL], preferred_element_type=F32)
    return mixed * (1.0 / total)


def attend_kernel(lengths, moves, query, cache, new, out):
    half = N * GROUP
    rows = STEPS * GROUP
    body = REQ * rows
    turn = pl.program_id(0)
    for u in range(TOGETHER):
        request = turn * TOGETHER + u
        q = jnp.concatenate([query[s, u].T for s in range(STEPS)], axis=0)
        fresh = new[...].astype(F32)
        fresh = jnp.where(turn == 0, fresh[:, u, :], fresh[:, TOGETHER + u, :])
        own = jnp.concatenate([fresh, jnp.zeros((META - STEPS, fresh.shape[1]), F32)], axis=0)
        mixed = attend_one(q, cache[u], own.astype(BF16), lengths[request])
        mixed = jnp.concatenate(
            [mixed[:half].reshape(N, GROUP, VAL), mixed[half:].reshape(N, GROUP, VAL)], axis=1
        ).astype(BF16)
        for p in range(VAL // LANES):
            at = pl.multiple_of(p * body + request * rows, rows)
            out[:, pl.ds(at, rows), :] = mixed[:, :, p * LANES : (p + 1) * LANES]
    lane = lax.broadcasted_iota(jnp.int32, (N, META, LANES), 2)
    slot = moves[0, 0]
    taker = jnp.where(slot < REQ, moves[0, 1], -1)
    out[:, body * (VAL // LANES) :, :] = (
        jnp.where(lane < LANES // 2, taker, slot).astype(F32).astype(BF16)
    )


def attend(lengths, moves, queries, cache, new):
    width = cache.shape[1]
    rows = REQ * STEPS * GROUP * (VAL // LANES) + META
    return pl.pallas_call(
        attend_kernel,
        grid_spec=pltpu.PrefetchScalarGridSpec(
            num_scalar_prefetch=2,
            grid=(REQ // TOGETHER,),
            in_specs=[
                pl.BlockSpec((STEPS, TOGETHER, width, N * GROUP), lambda g, *_: (0, g, 0, 0)),
                pl.BlockSpec((TOGETHER, width, cache.shape[2]), lambda g, *_: (g, 0, 0)),
                pl.BlockSpec(new.shape, lambda g, *_: (0, 0, 0)),
            ],
            out_specs=pl.BlockSpec((N, rows, LANES), lambda g, *_: (0, 0, 0)),
        ),
        out_shape=jax.ShapeDtypeStruct((N, rows, LANES), BF16),
        compiler_params=pltpu.CompilerParams(vmem_limit_bytes=56 * 2**20),
    )(lengths, moves, queries, cache, new)


def value_kernel(got, weight, *refs):
    outs, wide = refs[:-1], refs[-1]
    body = REQ * STEPS * GROUP
    pieces = VAL // LANES
    moves = got[:, pieces * body :, :].astype(F32)[:, 0, :]
    sub = lax.broadcasted_iota(jnp.int32, (N, LANES), 0)
    lane = lax.broadcasted_iota(jnp.int32, (N, LANES), 1)
    taker = jnp.max(jnp.where(lane < LANES // 2, moves, -1.0), axis=1, keepdims=True)
    slot = jnp.max(jnp.where(lane < LANES // 2, -1.0, moves), axis=1, keepdims=True)
    parts = []
    for (first, count), out in zip(CHUNKS, outs, strict=True):
        cell = count * STEPS * GROUP
        home = N * count * STEPS
        for p in range(pieces):
            at = p * body + first * STEPS * GROUP
            wide[p, : N * cell, :] = got[:, at : at + cell, :].astype(F32).reshape(N * cell, LANES)
        for h in range(GROUP):
            rows = jnp.concatenate(
                [wide[p, pl.ds(h, home, stride=GROUP), :] for p in range(pieces)], axis=1
            ).astype(BF16)
            out[h * home : (h + 1) * home, :] = jnp.dot(
                rows, weight[h], preferred_element_type=F32
            ).astype(BF16)
        mine = lane // (count * STEPS) == sub
        for v in (taker, slot):
            parts.append(jnp.sum(jnp.where(mine, v, 0.0), axis=0, keepdims=True))
    row = lax.broadcasted_iota(jnp.int32, (META, LANES), 0)
    lines = jnp.zeros((META, LANES), F32)
    for i, part in enumerate(parts):
        lines = jnp.where(row == i, part, lines)
    out[GROUP * home :, :] = lines.astype(BF16)


def values(got, weight):
    homes = [N * count * STEPS for _, count in CHUNKS]
    shapes = [(h * GROUP + (META if p == len(homes) - 1 else 0), HEAD) for p, h in enumerate(homes)]
    whole = [pl.BlockSpec(s, lambda g: (0, 0)) for s in shapes]
    return pl.pallas_call(
        value_kernel,
        grid=(1,),
        in_specs=[
            pl.BlockSpec(got.shape, lambda g: (0, 0, 0)),
            pl.BlockSpec(weight.shape, lambda g: (0, 0, 0)),
        ],
        out_specs=whole,
        out_shape=[jax.ShapeDtypeStruct(s, BF16) for s in shapes],
        scratch_shapes=[pltpu.VMEM((VAL // LANES, max(homes) * GROUP, LANES), F32)],
        compiler_params=pltpu.CompilerParams(vmem_limit_bytes=24 * 2**20),
    )(got, weight)


def pack(rows):
    full = rows.shape[2] // LANES
    half = rows.shape[1] // 2
    tail = rows[:, :, full * LANES :]
    return [rows[:, :, t * LANES : (t + 1) * LANES] for t in range(full)] + [
        jnp.concatenate([tail[:, :half], tail[:, half:]], axis=2)
    ]


def unpack(packed, count):
    half = count // 2
    full = (packed.shape[0] - half) // count
    tail = packed[full * count :]
    tail = jnp.concatenate([tail[:, : LANES // 2], tail[:, LANES // 2 :]], axis=0)
    return jnp.concatenate([packed[t * count : (t + 1) * count] for t in range(full)] + [tail], axis=1)


def put(out, parts):
    at = 0
    for part in parts:
        out[:, at : at + part.shape[1], :] = part.astype(BF16)
        at += part.shape[1]


def project_kernel(order, *refs):
    blocks, (weight, out, table_out, held, taps, staged, extra, sem) = refs[:N], refs[N:]
    fill = pltpu.make_async_copy(weight, taps, sem.at[2 * N])
    fill.start()
    copies = [
        pltpu.make_async_copy(block, held.at[b], sem.at[b]) for b, block in enumerate(blocks)
    ]
    for copy in copies:
        copy.start()
    fill.wait()
    cols = taps.shape[0]
    size = staged.shape[1]
    lane = lax.broadcasted_iota(jnp.int32, (1, HOME), 1)
    sub = lax.broadcasted_iota(jnp.int32, (N, HOME), 0)
    table = jnp.zeros((N, HOME), F32)
    sends, halves, codes = [], [], []
    for first in range(0, N, AT_ONCE):
        for copy in copies[first : first + AT_ONCE]:
            copy.wait()
        depth = [
            held[first : first + AT_ONCE, h * HOME : (h + 1) * HOME, :].reshape(AT_ONCE * HOME, HEAD)
            for h in range(GROUP)
        ]
        rows = lax.dot_general(
            jnp.concatenate(depth, axis=1), taps[...], NT, preferred_element_type=F32
        )
        at = 0
        for part in pack(rows.reshape(AT_ONCE, HOME, cols)):
            staged[first : first + AT_ONCE, at : at + part.shape[1], :] = part.astype(BF16)
            at += part.shape[1]
        for b in range(first, first + AT_ONCE):
            send = pltpu.make_async_copy(
                staged.at[b], out.at[order[b], pl.ds(0, size)], sem.at[N + b]
            )
            send.start()
            sends.append(send)
            line = held[b, GROUP * HOME :, :].astype(F32)
            table = jnp.where(sub == order[b], line[1:2], table)
            line = line.astype(jnp.int32)
            here = line[1:2] == (lane % CELL) // STEPS
            codes.append(jnp.where(here, (line[0:1] * N + lane // CELL) * STEPS + lane % STEPS, -1))
        halves.append(rows.astype(BF16))
    table_out[...] = table
    came = jnp.zeros((N * ARRIVING, cols), F32)
    for g, rows in enumerate(halves):
        wanted = jnp.concatenate(codes[g * AT_ONCE : (g + 1) * AT_ONCE], axis=1)
        r = lax.broadcasted_iota(jnp.int32, (N * ARRIVING, wanted.shape[1]), 0)
        pick = (r == wanted).astype(F32).astype(BF16)
        came = came + jnp.dot(pick, rows, preferred_element_type=F32)
    at = 0
    for part in pack(came.reshape(N, ARRIVING, cols)):
        extra[:, at : at + part.shape[1], :] = part.astype(BF16)
        at += part.shape[1]
    rest = pltpu.make_async_copy(extra, out.at[:, pl.ds(size, extra.shape[1])], sem.at[2 * N + 1])
    rest.start()
    sends.append(rest)
    for send in sends:
        send.wait()


def project(order, blocks, weight):
    cols = weight.shape[0]
    packed = HOME * cols // LANES
    added = ARRIVING * cols // LANES
    hbm = pl.BlockSpec(memory_space=pltpu.HBM)
    return pl.pallas_call(
        project_kernel,
        grid_spec=pltpu.PrefetchScalarGridSpec(
            num_scalar_prefetch=1,
            grid=(1,),
            in_specs=[hbm] * (N + 1),
            out_specs=[hbm, pl.BlockSpec((N, HOME), lambda g, *_: (0, 0))],
            scratch_shapes=[
                pltpu.VMEM((N,) + blocks[0].shape, BF16),
                pltpu.VMEM(weight.shape, BF16),
                pltpu.VMEM((N, packed, LANES), BF16),
                pltpu.VMEM((N, added, LANES), BF16),
                pltpu.SemaphoreType.DMA((2 * N + 2,)),
            ],
        ),
        out_shape=[
            jax.ShapeDtypeStruct((N, packed + added, LANES), BF16),
            jax.ShapeDtypeStruct((N, HOME), F32),
        ],
        compiler_params=pltpu.CompilerParams(vmem_limit_bytes=50 * 2**20),
    )(order, *blocks, weight)


def finish_kernel(mine, table, got, out):
    total = got[0].astype(F32)
    for j in range(1, N):
        total = total + got[j].astype(F32)
    size, cols = out.shape
    packed = HOME * cols // LANES
    rows = jnp.concatenate(
        [unpack(total[:packed], HOME), unpack(total[packed:], ARRIVING)], axis=0
    ).astype(BF16)
    o = lax.broadcasted_iota(jnp.int32, (size, size), 0)
    col = lax.broadcasted_iota(jnp.int32, (size, size), 1)
    slots = REQ + 1
    step, j, slot = o // (N * slots), (o // slots) % N, o % slots
    source = jnp.where(slot < REQ, j * CELL + slot * STEPS + step, HOME + j * STEPS + step)
    line = table[...]
    row = lax.broadcasted_iota(jnp.int32, line.shape, 0)
    line = jnp.sum(jnp.where(row == mine[0], line, 0.0), axis=0, keepdims=True)
    r = lax.broadcasted_iota(jnp.int32, (size, HOME), 0)
    lane = lax.broadcasted_iota(jnp.int32, (size, HOME), 1)
    pick_slot = ((r // slots) % N) * CELL == lane
    away = jnp.sum(jnp.where(pick_slot, line, 0.0), axis=1, keepdims=True)
    slot_of = lax.broadcasted_iota(jnp.int32, (size, 1), 0) % slots
    stays = (slot_of == REQ) | (slot_of.astype(F32) != away)
    pick = ((col == source) & stays).astype(F32).astype(BF16)
    out[...] = jnp.dot(pick, rows, preferred_element_type=F32).astype(BF16)


def finish(mine, table, got, cols):
    vmem = pl.BlockSpec(memory_space=pltpu.VMEM)
    return pl.pallas_call(
        finish_kernel,
        in_specs=[pl.BlockSpec(memory_space=pltpu.SMEM), vmem, vmem],
        out_specs=vmem,
        out_shape=jax.ShapeDtypeStruct((HOME + ARRIVING, cols), BF16),
        compiler_params=pltpu.CompilerParams(vmem_limit_bytes=16 * 2**20),
    )(mine, table, got)


def along_z(by):
    chips = N // 2
    return [(z * 2 + c, (z + by) % chips * 2 + c) for z in range(chips) for c in range(2)]


OTHER_CORE = [(i, i ^ 1) for i in range(N)]


def gather(block):
    me = lax.axis_index("dp")
    chips = N // 2
    held = [(block, me)]
    up = down = block
    for hop in range(1, chips // 2 + 1):
        up = lax.ppermute(up, "dp", along_z(1))
        held.append((up, (me + N - 2 * hop) % N))
        if hop < chips // 2:
            down = lax.ppermute(down, "dp", along_z(-1))
            held.append((down, (me + 2 * hop) % N))
    held += [(lax.ppermute(b, "dp", OTHER_CORE), i ^ 1) for b, i in held]
    return [b for b, _ in held], jnp.stack([i for _, i in held]).astype(jnp.int32)


def across_tp(x):
    return lax.all_to_all(x, "tp", split_axis=0, concat_axis=0, tiled=True)


def shards(latent_cache, lengths, queries, new_latents, migrations, value_weight, output_weight):
    cache = jnp.swapaxes(latent_cache, 1, 2)
    asked = jnp.swapaxes(queries, 2, 3)
    weight = jnp.swapaxes(output_weight, 0, 1)
    sent = attend(lengths, migrations, asked, cache, new_latents)
    hidden = values(across_tp(sent), value_weight)
    blocks, order = gather(hidden[0])
    partial, table = project(order, blocks, weight)
    mine = lax.axis_index("tp").astype(jnp.int32).reshape(1)
    partial, table, mine = lax.optimization_barrier((partial, table, mine))
    shares = across_tp(partial)
    return finish(mine, table, shares, weight.shape[0])


def solution(mesh):
    return jax.shard_map(
        shards,
        mesh=mesh,
        in_specs=(
            P(("dp", "tp"), None, None),
            P(("dp", "tp")),
            P(None, ("dp", "tp"), None, None),
            P(None, ("dp", "tp"), None),
            P(("dp", "tp"), None),
            P("tp", None, None),
            P("tp", "dp"),
        ),
        out_specs=P("tp", "dp"),
        check_vma=False,
    )
```
